512 devices in a mesh: gx: 32 (over z, core), gy: 16 (over y, x).
Axes of the slice: x: 4, y: 4, z: 16, core: 2. Of those that a mesh axis runs over, the one named last changes fastest.
Arguments:
- rhs_leaf: float32 [32, 16, 8, 512], P('gx', 'gy'), may hold values from -6 to 6
- leaf_inv: float32 [32, 16, 4, 128, 128], P('gx', 'gy'), may hold values from -0.5 to 0.5
- leaf_sub: float32 [32, 16, 3, 128, 128], P('gx', 'gy'), may hold values from -0.375 to 0.375
- sep_rhs: float32 [32, 16, 8, 96], P('gx', 'gy'), may hold values from -6 to 6
- interface: int32 [32, 16, 4, 128], P('gx', 'gy'), may hold values from 0 to 8191, as said below
- coupling: float32 [32, 16, 4, 128, 512], P('gx', 'gy'), may hold values from -0.125 to 0.125
- factor_one: float32 [32, 16, 16, 8192], P('gx', 'gy'), may hold values from -0.0625 to 0.0625
- factor_two: float32 [32, 16, 16, 4096], P('gx', 'gy'), may hold values from -0.09375 to 0.09375
- factor_three: float32 [32, 16, 32, 4096], P('gx', 'gy'), may hold values from -0.09375 to 0.09375
- factor_four: float32 [32, 16, 32, 2048], P('gx', 'gy'), may hold values from -0.125 to 0.125
- link_two: float32 [32, 16, 16, 128], P('gx', 'gy'), may hold values from -0.375 to 0.375
- link_three: float32 [32, 16, 32, 128], P('gx', 'gy'), may hold values from -0.25 to 0.25
- link_four: float32 [32, 16, 32, 128], P('gx', 'gy'), may hold values from -0.25 to 0.25
Outputs:
- leaf_solution: float32 [32, 16, 8, 512], P('gx', 'gy')
- sep_solution: float32 [32, 16, 8, 96], P('gx', 'gy')
The draws below stay inside these ranges and needn't reach their ends.
Inputs may be any that keep to these rules, and one draw needn't show every extreme that they name: interface[a, c, k-1, n] is a position of a level-k separator, below S_k, and S_k - 1 is reached at every level; positions may repeat within a leaf.
All inputs are finite; a program needn't handle non-finite values.
Results may differ from the reference program's by a relative error of at most 0.00014.
Values sent between devices are 32-bit elements; how exact they have to be, the bound alone decides.
A program may use at most 64 MiB of HBM per device.

```python
import jax
import jax.numpy as jnp
import numpy as np
from jax import lax

R = 8
BL = 128
NB = 4
NIF = 128
SROWS = 16
NL = 512
BLOCKS_X = 32
BLOCKS_Y = 16
SEP1 = 8192
SEP2 = 4096
SEP3 = 4096
SEP4 = 2048
ALLROWS = 96
N_GX = 32
N_GY = 16


def draw_interface(key, part):
    tops = [SEP1, SEP2, SEP3, SEP4]
    columns = []
    for section in range(4):
        values = jax.random.randint(jax.random.fold_in(key, 101 + section), (BLOCKS_X, BLOCKS_Y, NIF), 0, tops[section], dtype=jnp.int32)
        values = values.at[0, 0, 0].set(tops[section] - 1)
        values = values.at[0, 0, 1].set(0)
        columns.append(values)
    return jnp.stack(columns, axis=2)


def block_scale(own_key, extent, cuts, smallest, largest):
    loudness = 1.0
    for axis_at, shards_of in cuts:
        steps = jax.random.uniform(jax.random.fold_in(jax.random.fold_in(own_key, 6), axis_at), (shards_of,), jnp.float32, smallest / len(cuts), largest / len(cuts))
        loudness = loudness * jnp.repeat(jnp.exp(steps), extent[axis_at] // shards_of).reshape((-1,) + (1,) * (len(extent) - 1 - axis_at))
    return loudness


def normal_values(rng, dims, width, reach, split=(), kind=jnp.bfloat16):
    loudness = block_scale(rng, dims, split, -0.22, 0.18) if split else 1.0
    drawn = jax.random.normal(rng, dims, jnp.float32) * width * loudness
    return jnp.minimum(jnp.maximum(drawn, -reach), reach).astype(kind)


def setup_inputs(seed: int = 0) -> dict:
    arg_keys = jax.random.split(jax.random.key(seed), 14)
    rhs_leaf = normal_values(arg_keys[0], (BLOCKS_X, BLOCKS_Y, R, NL), 1.0, 6.0, ((0, 32), (1, 16)), jnp.float32)
    leaf_inv = normal_values(arg_keys[1], (BLOCKS_X, BLOCKS_Y, NB, BL, BL), BL ** -0.5, 0.5, ((0, 32), (1, 16)), jnp.float32)
    leaf_sub = normal_values(arg_keys[2], (BLOCKS_X, BLOCKS_Y, NB - 1, BL, BL), (2 * BL) ** -0.5, 0.375, ((0, 32), (1, 16)), jnp.float32)
    sep_rhs = normal_values(arg_keys[3], (BLOCKS_X, BLOCKS_Y, R, ALLROWS), 1.0, 6.0, ((0, 32), (1, 16)), jnp.float32)
    interface = draw_interface(jax.random.fold_in(arg_keys[13], 71), 0)
    coupling = normal_values(arg_keys[5], (BLOCKS_X, BLOCKS_Y, 4, NIF, NL), (4 * NL) ** -0.5, 0.125, ((0, 32), (1, 16)), jnp.float32)
    factor_one = normal_values(arg_keys[6], (BLOCKS_X, BLOCKS_Y, SROWS, SEP1), SEP1 ** -0.5, 0.0625, ((0, 32), (1, 16)), jnp.float32)
    factor_two = normal_values(arg_keys[7], (BLOCKS_X, BLOCKS_Y, SROWS, SEP2), SEP2 ** -0.5, 0.09375, ((0, 32), (1, 16)), jnp.float32)
    factor_three = normal_values(arg_keys[8], (BLOCKS_X, BLOCKS_Y, 2 * SROWS, SEP3), SEP3 ** -0.5, 0.09375, ((0, 32), (1, 16)), jnp.float32)
    factor_four = normal_values(arg_keys[9], (BLOCKS_X, BLOCKS_Y, 2 * SROWS, SEP4), SEP4 ** -0.5, 0.125, ((0, 32), (1, 16)), jnp.float32)
    link_two = normal_values(arg_keys[10], (BLOCKS_X, BLOCKS_Y, SROWS, NIF), (16 * SROWS) ** -0.5, 0.375, ((0, 32), (1, 16)), jnp.float32)
    link_three = normal_values(arg_keys[11], (BLOCKS_X, BLOCKS_Y, 2 * SROWS, NIF), (32 * SROWS) ** -0.5, 0.25, ((0, 32), (1, 16)), jnp.float32)
    link_four = normal_values(arg_keys[12], (BLOCKS_X, BLOCKS_Y, 2 * SROWS, NIF), (32 * SROWS) ** -0.5, 0.25, ((0, 32), (1, 16)), jnp.float32)
    return {"rhs_leaf": rhs_leaf, "leaf_inv": leaf_inv, "leaf_sub": leaf_sub, "sep_rhs": sep_rhs, "interface": interface, "coupling": coupling, "factor_one": factor_one, "factor_two": factor_two, "factor_three": factor_three, "factor_four": factor_four, "link_two": link_two, "link_three": link_three, "link_four": link_four}


PRECISE = lax.Precision.HIGHEST


def taken_lists():
    gy_bits = N_GY.bit_length() - 1
    gx_bits = N_GX.bit_length() - 1
    first = list(range(gy_bits + gx_bits))
    second = [bit_number for bit_number in first if bit_number != gy_bits + gx_bits - 1]
    third = [bit_number for bit_number in second if bit_number != gy_bits - 1]
    fourth = [bit_number for bit_number in third if bit_number != gy_bits + gx_bits - 2]
    return [first, second, third, fourth]


def group_tables(taken):
    device_ids = np.arange(N_GX * N_GY)
    group_rank = device_ids * 0
    for bit_number in sorted(taken, reverse=True):
        group_rank = group_rank * 2 + ((device_ids >> bit_number) & 1)
    taken_mask = 0
    for bit_number in taken:
        taken_mask = taken_mask + (1 << bit_number)
    group_keys, group_of = np.unique(device_ids & (~taken_mask), return_inverse=True)
    return group_rank, group_of.reshape(-1), len(group_keys)


def leaf_forward(right_side, inverse_blocks, lower_blocks):
    results = []
    earlier = None
    for counter in range(NB):
        current = right_side[:, :, counter * BL:(counter + 1) * BL]
        if counter > 0:
            current = current - jnp.einsum('drk,dkl->drl', earlier, lower_blocks[:, counter - 1], precision=PRECISE)
        earlier = jnp.einsum('drk,dkl->drl', current, inverse_blocks[:, counter], precision=PRECISE)
        results.append(earlier)
    return jnp.concatenate(results, axis=2)


def leaf_backward(leaf_work, inverse_blocks, lower_blocks):
    results = [None] * NB
    later = None
    for counter in reversed(range(NB)):
        current = leaf_work[:, :, counter * BL:(counter + 1) * BL]
        if counter < NB - 1:
            current = current - jnp.einsum('drl,dkl->drk', later, lower_blocks[:, counter], precision=PRECISE)
        later = jnp.einsum('drl,dkl->drk', current, inverse_blocks[:, counter], precision=PRECISE)
        results[counter] = later
    return jnp.concatenate(results, axis=2)


def reference(rhs_leaf, leaf_inv, leaf_sub, sep_rhs, interface, coupling, factor_one, factor_two, factor_three, factor_four, link_two, link_three, link_four):
    devices = N_GX * N_GY

    def flatten(array):
        return array.reshape((devices,) + array.shape[2:])

    factors = [flatten(factor_one), flatten(factor_two), flatten(factor_three), flatten(factor_four)]
    link_mats = [flatten(link_two), flatten(link_three), flatten(link_four)]
    places = flatten(interface)
    couplings = flatten(coupling)
    own_rhs = flatten(sep_rhs)
    inverse_blocks = flatten(leaf_inv)
    lower_blocks = flatten(leaf_sub)
    row_counts = [SROWS, SROWS, 2 * SROWS, 2 * SROWS]
    sep_widths = [SEP1, SEP2, SEP3, SEP4]
    offsets = [0, SROWS, 2 * SROWS, 4 * SROWS]
    group_index = []
    owned = []
    group_counts = []
    for taken in taken_lists():
        group_rank, group_of, group_count = group_tables(taken)
        group_index.append(jnp.asarray(group_of, dtype=jnp.int32)[:, None])
        own_rows = row_counts[len(owned)]
        owned.append(jnp.asarray(group_rank[:, None] * own_rows + np.arange(own_rows)[None, :], dtype=jnp.int32))
        group_counts.append(group_count)
    forward = leaf_forward(flatten(rhs_leaf), inverse_blocks, lower_blocks)
    own_z = [None] * 4
    for section in (3, 2, 1, 0):
        own_rows = row_counts[section]
        partials_in = jnp.einsum('drl,dnl->drn', forward, couplings[:, section], precision=PRECISE)
        if section < 3:
            partials_in = partials_in + jnp.einsum('drq,dqn->drn', own_z[section + 1], link_mats[section], precision=PRECISE)
        summed = jnp.zeros((group_counts[section], R, sep_widths[section]), jnp.float32)
        own_part = own_rhs[:, :, offsets[section]:offsets[section] + own_rows]
        summed = summed.at[group_index[section], :, owned[section]].add(jnp.transpose(own_part, (0, 2, 1)))
        summed = summed.at[group_index[section], :, places[:, section]].add(-jnp.transpose(partials_in, (0, 2, 1)))
        own_z[section] = jnp.einsum('drs,dqs->drq', summed[group_index[section][:, 0]], factors[section], precision=PRECISE)
    full_sep = [None] * 4
    own_x = []
    for section in range(4):
        update = own_z[section]
        if section > 0:
            picked = full_sep[section - 1][group_index[section - 1], :, places[:, section - 1]]
            update = update - jnp.einsum('dnr,dqn->drq', picked, link_mats[section - 1], precision=PRECISE)
        partial_value = jnp.einsum('drq,dqs->drs', update, factors[section], precision=PRECISE)
        full_sep[section] = jax.ops.segment_sum(partial_value, group_index[section][:, 0], num_segments=group_counts[section])
        own_x.append(jnp.transpose(full_sep[section][group_index[section], :, owned[section]], (0, 2, 1)))
    leaf_work = forward
    for section in range(4):
        picked = full_sep[section][group_index[section], :, places[:, section]]
        leaf_work = leaf_work - jnp.einsum('dnr,dnl->drl', picked, couplings[:, section], precision=PRECISE)
    leaf_solution = leaf_backward(leaf_work, inverse_blocks, lower_blocks)
    sep_solution = jnp.concatenate(own_x, axis=2)
    return leaf_solution.reshape(N_GX, N_GY, R, NL), sep_solution.reshape(N_GX, N_GY, R, 6 * SROWS)
```

```python
import functools

import jax
import jax.numpy as jnp
from jax import lax
from jax.experimental import pallas as pl
from jax.experimental.pallas import tpu as pltpu
from jax.sharding import PartitionSpec as P

MESH = pl.DeviceIdType.MESH
F32 = jnp.float32
BF16 = jnp.bfloat16
HIGHEST = lax.Precision.HIGHEST
NN = (((1,), (0,)), ((), ()))
NT = (((1,), (1,)), ((), ()))
TILE = 128
NX, NY, NC, NZ = 4, 4, 2, 16


def dense(a, b, dims=NN):
    return lax.dot_general(a, b, dims, precision=HIGHEST, preferred_element_type=F32)


def fast(a, b, dims=NN):
    return lax.dot_general(a, b, dims, preferred_element_type=F32)


def halves(v):
    high = v.astype(BF16).astype(F32)
    return high, v - high


class Level:
    def __init__(self, own, width, off, ny, nz, scatter, exchange):
        self.own = own
        self.width = width
        self.tiles = width // TILE
        self.off = off
        self.size = {"x": NX, "y": ny, "c": NC, "z": nz}
        self.scatter = scatter
        self.exchange = exchange
        self.n_scatter = self.count(scatter)
        self.n_exchange = self.count(exchange)
        self.share = self.tiles // self.n_scatter

    def count(self, axes):
        n = 1
        for axis in axes:
            n *= self.size[axis]
        return n

    def steps(self, axes):
        out = [{}]
        for axis in axes:
            out = [dict(o, **{axis: d}) for d in range(self.size[axis]) for o in out]
        return out[1:]


LEVELS = (
    Level(16, 8192, 0, 4, 16, "xyc", "z"),
    Level(16, 4096, 16, 4, 8, "xyc", "z"),
    Level(32, 4096, 32, 2, 8, "xyc", "z"),
    Level(32, 2048, 64, 2, 4, "xc", "yz"),
)


def kernel(
    rhs_h, inv_h, sub_h, sep_h, pos_h, cpl_h, f1_h, f2_h, f3_h, f4_h, l2_h, l3_h, l4_h,
    leaf_out, sep_out,
    rhs, inv, sub, sep, pos, cpl, f1, f2, f3, f4, l2, l3, l4,
    fwd, base, place_t, place, owned, zval, vmat, cv, work,
    *rest,
):
    bufs = rest[:8]
    in_sem, send_sem, recv_sem = rest[8][0], rest[8][1], rest[8][2]
    factors = (f1, f2, f3, f4)
    links = (l2, l3, l4)

    a, c = lax.axis_index("gx"), lax.axis_index("gy")
    index = a * 16 + c
    here = {"x": lax.rem(c, 4), "y": lax.div(c, 4), "c": lax.rem(a, 2), "z": lax.div(a, 2)}

    def moved(level, step):
        there = dict(here)
        for axis, d in step.items():
            if d:
                n = level.size[axis]
                v = here[axis]
                full = {"x": NX, "y": NY, "c": NC, "z": NZ}[axis]
                if n == full:
                    there[axis] = lax.rem(v + d, n)
                else:
                    inside = lax.rem(v, n)
                    there[axis] = v - inside + lax.rem(inside + d, n)
        return there

    def device(there):
        return (there["z"] * 2 + there["c"], there["y"] * 4 + there["x"])

    def share_of(level, there):
        r = 0
        for axis in level.scatter:
            r = r * level.size[axis] + lax.rem(there[axis], level.size[axis])
        return r

    low = lax.rem(index, 256)
    ranks = (
        index,
        low,
        lax.div(low, 16) * 8 + lax.rem(index, 8),
        lax.div(lax.rem(index, 128), 16) * 8 + lax.rem(index, 8),
    )

    pairs = (
        (rhs_h, rhs), (inv_h, inv), (sub_h, sub), (pos_h, pos), (cpl_h, cpl), (sep_h, sep),
        (f4_h, f4), (l4_h, l4), (f3_h, f3), (l3_h, l3), (f2_h, f2), (l2_h, l2), (f1_h, f1),
    )
    copies = [pltpu.make_async_copy(s, d, in_sem.at[n]) for n, (s, d) in enumerate(pairs)]
    for copy in copies:
        copy.start()

    barrier = pltpu.get_barrier_semaphore()
    greet = {}
    for level in LEVELS:
        for axes in (level.exchange, level.scatter):
            for step in level.steps(axes):
                key = (axes, tuple(sorted(step.items())))
                if axes == "z" and level.size["z"] < NZ:
                    continue
                if axes == "xyc" and level.size["y"] < NY:
                    continue
                if axes == "xc":
                    continue
                if axes == "yz" and (step["y"] == 0):
                    continue
                if axes == "yz" and (step["z"] == 0):
                    continue
                greet[key] = (level, step)
    for level, step in greet.values():
        pl.semaphore_signal(barrier, inc=1, device_id=device(moved(level, step)), device_id_type=MESH)

    for n in range(3):
        copies[n].wait()
    earlier = None
    for j in range(4):
        current = rhs[:, j * TILE : (j + 1) * TILE]
        if j:
            current = current - dense(earlier, sub[j - 1])
        earlier = dense(current, inv[j])
        fwd[:, j * TILE : (j + 1) * TILE] = earlier
    for n in range(3, 6):
        copies[n].wait()

    def prepare(k):
        level = LEVELS[k]
        row = pos[k : k + 1, :]
        lane = lax.rem(row, TILE)
        hot = jnp.broadcast_to(lane, (TILE, TILE)) == lax.broadcasted_iota(jnp.int32, (TILE, TILE), 0)
        hot = jnp.where(hot, 1.0, 0.0)
        turned = jnp.transpose(hot).astype(BF16)
        hot = hot.astype(BF16)
        place_t[k] = jnp.concatenate([hot, hot], axis=0)
        place[k] = jnp.concatenate([turned, turned], axis=0)
        base[k] = dense(fwd[...], cpl[k], NT)
        owned[k] = dense(sep[...], select(k))

    def select(k):
        level = LEVELS[k]
        start = lax.rem(ranks[k] * level.own, TILE)
        q = lax.broadcasted_iota(jnp.int32, (96, TILE), 0) - level.off
        lane = lax.broadcasted_iota(jnp.int32, (96, TILE), 1)
        hit = (q + start == lane) & (q >= 0) & (q < level.own)
        return jnp.where(hit, 1.0, 0.0)

    def tile_of(k):
        row = jnp.broadcast_to(lax.div(pos[k : k + 1, :], TILE), (8, TILE))
        tiles = LEVELS[k].tiles
        return jnp.broadcast_to(row[None], (tiles, 8, TILE)) == lax.broadcasted_iota(
            jnp.int32, (tiles, 8, TILE), 0
        )

    def own_tile(k):
        return lax.div(ranks[k] * LEVELS[k].own, TILE)

    def scatter(k, term, out):
        tiles = LEVELS[k].tiles
        hit = tile_of(k)
        high, lo = halves(-term)
        parts = [
            jnp.where(hit, jnp.broadcast_to(v[None], (tiles, 8, TILE)), 0.0).reshape(tiles * 8, TILE).astype(BF16)
            for v in (high, lo)
        ]
        out[...] = fast(jnp.concatenate(parts, axis=1), place[k]).reshape(tiles, 8, TILE)
        at = pl.ds(own_tile(k), 1)
        out[at] = out[at] + owned[k][None]

    def gather(k, full):
        tiles = LEVELS[k].tiles
        high, lo = halves(full[...].reshape(tiles * 8, TILE))
        got = fast(jnp.concatenate([high.astype(BF16), lo.astype(BF16)], axis=1), place_t[k])
        return jnp.sum(jnp.where(tile_of(k), got.reshape(tiles, 8, TILE), 0.0), axis=0)

    def remote(src, dst, slot, phase, target):
        return pltpu.make_async_remote_copy(
            src_ref=src, dst_ref=dst, send_sem=send_sem.at[slot, phase], recv_sem=recv_sem.at[slot, phase],
            device_id=target, device_id_type=MESH,
        )

    me = (a, c)
    leftover = []

    def total(k, slot, beside=(None, None, None)):
        level = LEVELS[k]
        w = level.share
        part, got, mine, seen, full = bufs[2 * k + slot]
        s = 2 * k + slot
        own = share_of(level, here)
        peers = [moved(level, step) for step in level.steps(level.scatter)]
        for n, there in enumerate(peers):
            remote(part.at[pl.ds(share_of(level, there) * w, w)], got.at[n], s, 0, device(there)).start()
        if beside[0]:
            beside[0]()
        remote(got, got, s, 0, me).wait_recv()
        value = part[pl.ds(own * w, w)] + jnp.sum(got[...], axis=0)
        mine[...] = value
        for n, step in enumerate(level.steps(level.exchange)):
            remote(mine, seen.at[n], s, 1, device(moved(level, step))).start()
        if beside[1]:
            beside[1]()
        remote(seen, seen, s, 1, me).wait_recv()
        at = pl.ds(own * w, w)
        full[at] = mine[...] + jnp.sum(seen[...], axis=0)
        for there in peers:
            remote(full.at[at], full.at[at], s, 2, device(there)).start()
        if beside[2]:
            beside[2]()
        rest_of = full.at[pl.ds(0, level.tiles - w)]
        remote(rest_of, rest_of, s, 2, me).wait_recv()

        def finish():
            remote(rest_of, rest_of, s, 0, me).wait_send()
            remote(seen, seen, s, 1, me).wait_send()
            remote(got, got, s, 2, me).wait_send()

        leftover.append(finish)

    def times_rows(k, full):
        factor = factors[k]
        m = LEVELS[k].own

        def body(j, sums):
            tile = full[j]
            rows = factor[:, pl.ds(pl.multiple_of(j * TILE, TILE), TILE)]
            return tuple(sums[q] + tile * rows[q : q + 1, :] for q in range(m))

        sums = lax.fori_loop(0, LEVELS[k].tiles, body, tuple(jnp.zeros((8, TILE), F32) for _ in range(m)), unroll=4)
        return [jnp.sum(v, axis=1, keepdims=True) for v in sums]

    def spread(k, values, out):
        factor = factors[k]
        m = LEVELS[k].own
        wide = [jnp.broadcast_to(v, (8, TILE)) for v in values]

        def body(j, _):
            rows = factor[:, pl.ds(pl.multiple_of(j * TILE, TILE), TILE)]
            acc = wide[0] * rows[0:1, :]
            for q in range(1, m):
                acc = acc + wide[q] * rows[q : q + 1, :]
            out[j] = acc
            return 0

        lax.fori_loop(0, LEVELS[k].tiles, body, 0, unroll=4)

    def inverse_blocks():
        vmat[...] = jnp.zeros_like(vmat)
        for j in range(4):
            vmat[j * TILE : (j + 1) * TILE, j * TILE : (j + 1) * TILE] = inv[j]
        for j in (2, 1, 0):
            step = -dense(inv[j], sub[j])
            vmat[j * TILE : (j + 1) * TILE, (j + 1) * TILE :] = dense(
                step, vmat[(j + 1) * TILE : (j + 2) * TILE, (j + 1) * TILE :]
            )

    def coupled():
        cv[...] = dense(cpl[3], vmat[...], NT)

    prepare(3)
    scatter(3, base[3], bufs[6][0])
    pl.semaphore_wait(barrier, len(greet))

    def others():
        for k in (2, 1, 0):
            prepare(k)

    besides = {3: (others, inverse_blocks, coupled)}
    first_copy = {3: 6, 2: 8, 1: 10, 0: 12}
    for k in (3, 2, 1, 0):
        total(k, 0, besides.get(k, (None, None, None)))
        m = LEVELS[k].own
        copies[first_copy[k]].wait()
        if k:
            copies[first_copy[k] + 1].wait()
        values = times_rows(k, bufs[2 * k][4])
        if k:
            term = base[k - 1]
            for q in range(m):
                term = term + values[q] * links[k - 1][q : q + 1, :]
            scatter(k - 1, term, bufs[2 * (k - 1)][0])
            for q in range(m):
                zval[LEVELS[k].off + q] = jnp.broadcast_to(values[q], (8, TILE))

    picked = None
    for k in range(4):
        m = LEVELS[k].own
        if k:
            values = [
                zval[LEVELS[k].off + q]
                - jnp.sum(picked * links[k - 1][q : q + 1, :], axis=1, keepdims=True)
                for q in range(m)
            ]
        spread(k, values, bufs[2 * k + 1][0])

        def after(k=k, picked=picked):
            if k == 0:
                work[...] = fwd[...]
                sep_out[...] = jnp.zeros_like(sep_out)
                return
            work[...] = work[...] - dense(picked, cpl[k - 1])
            sep_out[...] = sep_out[...] + dense(bufs[2 * k - 1][4][pl.ds(own_tile(k - 1), 1)][0], select(k - 1), NT)
            if k == 3:
                work[...] = dense(work[...], vmat[...], NT)

        total(k, 1, (after, None, None))
        picked = gather(k, bufs[2 * k + 1][4])
    leaf_out[...] = work[...] - dense(picked, cv[...])
    sep_out[...] = sep_out[...] + dense(bufs[7][4][pl.ds(own_tile(3), 1)][0], select(3), NT)
    for finish in leftover:
        finish()


def local(*args):
    ins = [x[0, 0] for x in args]
    order = ins
    vmem = [pltpu.VMEM(x.shape, x.dtype) for x in order]
    bufs = []
    for level in LEVELS:
        w = level.share
        shapes = (
            (level.tiles, 8, TILE),
            (level.n_scatter - 1, w, 8, TILE),
            (w, 8, TILE),
            (level.n_exchange - 1, w, 8, TILE),
            (level.tiles, 8, TILE),
        )
        for _ in range(2):
            bufs.append(tuple(pltpu.VMEM(s, F32) for s in shapes))
    scratch = vmem + [
        pltpu.VMEM((8, 512), F32),
        pltpu.VMEM((4, 8, TILE), F32),
        pltpu.VMEM((4, 2 * TILE, TILE), BF16),
        pltpu.VMEM((4, 2 * TILE, TILE), BF16),
        pltpu.VMEM((4, 8, TILE), F32),
        pltpu.VMEM((96, 8, TILE), F32),
        pltpu.VMEM((512, 512), F32),
        pltpu.VMEM((TILE, 512), F32),
        pltpu.VMEM((8, 512), F32),
    ]
    sems = (
        pltpu.SemaphoreType.DMA((13,)),
        pltpu.SemaphoreType.DMA((8, 3)),
        pltpu.SemaphoreType.DMA((8, 3)),
    )
    leaf, sep = pl.pallas_call(
        kernel,
        out_shape=(jax.ShapeDtypeStruct((8, 512), F32), jax.ShapeDtypeStruct((8, 96), F32)),
        in_specs=[pl.BlockSpec(memory_space=pl.ANY)] * len(ins),
        out_specs=(pl.BlockSpec(memory_space=pltpu.VMEM),) * 2,
        scratch_shapes=scratch + bufs + [sems],
        compiler_params=pltpu.CompilerParams(
            collective_id=0, has_side_effects=True, vmem_limit_bytes=40 * 1024 * 1024
        ),
        name="nested_solve",
    )(*ins)
    return leaf[None, None], sep[None, None]


def solution(mesh):
    four = P("gx", "gy", None, None)
    five = P("gx", "gy", None, None, None)
    in_specs = (four, five, five, four, four, five) + (four,) * 7
    return jax.shard_map(local, mesh=mesh, in_specs=in_specs, out_specs=(four, four), check_vma=False)
```

```python
import functools

import jax
import jax.numpy as jnp
from jax import lax
from jax.experimental import pallas as pl
from jax.experimental.pallas import tpu as pltpu
from jax.sharding import PartitionSpec as P

MESH = pl.DeviceIdType.MESH
F32 = jnp.float32
BF16 = jnp.bfloat16
HIGHEST = lax.Precision.HIGHEST
NN = (((1,), (0,)), ((), ()))
NT = (((1,), (1,)), ((), ()))
TILE = 128
NX, NY, NC, NZ = 4, 4, 2, 16


def dense(a, b, dims=NN):
    return lax.dot_general(a, b, dims, precision=HIGHEST, preferred_element_type=F32)


def fast(a, b, dims=NN):
    return lax.dot_general(a, b, dims, preferred_element_type=F32)


def halves(v):
    high = v.astype(BF16).astype(F32)
    return high, v - high


class Level:
    def __init__(self, own, width, off, scatter, exchange):
        self.own = own
        self.width = width
        self.tiles = width // TILE
        self.off = off
        self.scatter = scatter
        self.exchange = exchange
        self.share = self.tiles >> len(scatter)


LEVELS = (
    Level(16, 8192, 0, (0, 1, 2, 3, 4, 5), (6, 7, 8)),
    Level(16, 4096, 16, (0, 1, 2, 3, 4), (5, 6, 7)),
    Level(32, 4096, 32, (0, 1, 2, 4), (5, 6, 7)),
    Level(32, 2048, 64, (0, 1, 4), (2, 5, 6)),
)
SPARSE = (0, 1, 2, 5, 6)
CORE = (4,)


def hops(mask):
    def ring(n, m):
        return max(min(abs(v - (v ^ m)), n - abs(v - (v ^ m))) for v in range(n))

    return ring(4, mask & 3) + ring(4, mask >> 2 & 3) + ring(16, mask >> 5) + 0.1 * (mask >> 4 & 1)


def masks_of(bits):
    out = [0]
    for b in bits:
        out = out + [m | 1 << b for m in out]
    return sorted(out[1:], key=lambda m: (-hops(m), m))


def kernel(
    rhs_h, inv_h, sub_h, sep_h, pos_h, cpl_h, f1_h, f2_h, f3_h, f4_h, l2_h, l3_h, l4_h,
    leaf_out, sep_out,
    rhs, inv, sub, sep, pos, cpl, f1, f2, f3, f4, l2, l3, l4,
    fwd, base, place_t, place, owned, zval, vmat, cv, work,
    *rest,
):
    bufs = rest[:8]
    in_sem, send_sem, recv_sem = rest[8][0], rest[8][1], rest[8][2]
    factors = (f1, f2, f3, f4)
    links = (l2, l3, l4)

    a, c = lax.axis_index("gx"), lax.axis_index("gy")
    index = a * 16 + c
    bit = [lax.rem(lax.div(index, 1 << j), 2) for j in range(9)]
    flip = [1 - 2 * v for v in bit]

    def device(mask):
        x, y = a, c
        for j in range(9):
            if mask >> j & 1:
                if j < 4:
                    y = y + flip[j] * (1 << j)
                else:
                    x = x + flip[j] * (1 << (j - 4))
        return (x, y)

    def ordinal(bits, mask=0):
        r = 0
        for n, j in enumerate(bits):
            r = r + bit[j] * (1 << n)
            if mask >> j & 1:
                r = r + flip[j] * (1 << n)
        return r

    low = lax.rem(index, 256)
    ranks = (
        index,
        low,
        lax.div(low, 16) * 8 + lax.rem(index, 8),
        lax.div(lax.rem(index, 128), 16) * 8 + lax.rem(index, 8),
    )

    pairs = (
        (sep_h, sep), (pos_h, pos), (rhs_h, rhs), (inv_h, inv), (sub_h, sub),
        (cpl_h.at[3], cpl.at[3]), (cpl_h.at[pl.ds(0, 3)], cpl.at[pl.ds(0, 3)]),
        (f4_h, f4), (l4_h, l4), (f3_h, f3), (l3_h, l3), (f2_h, f2), (l2_h, l2), (f1_h, f1),
    )
    copies = [pltpu.make_async_copy(s, d, in_sem.at[n]) for n, (s, d) in enumerate(pairs)]
    for copy in copies:
        copy.start()

    barrier = pltpu.get_barrier_semaphore()
    greet = set(masks_of(SPARSE)) | set(masks_of(CORE))
    for level in LEVELS:
        greet |= set(masks_of(level.scatter)) | set(masks_of(level.exchange))
    for mask in sorted(greet, key=lambda m: (-hops(m), m)):
        pl.semaphore_signal(barrier, inc=1, device_id=device(mask), device_id_type=MESH)

    def prepare(k):
        level = LEVELS[k]
        row = pos[k : k + 1, :]
        lane = lax.rem(row, TILE)
        hot = jnp.broadcast_to(lane, (TILE, TILE)) == lax.broadcasted_iota(jnp.int32, (TILE, TILE), 0)
        hot = jnp.where(hot, 1.0, 0.0)
        turned = jnp.transpose(hot).astype(BF16)
        hot = hot.astype(BF16)
        place_t[k] = jnp.concatenate([hot, hot], axis=0)
        place[k] = jnp.concatenate([turned, turned], axis=0)
        if k < 3:
            base[k] = dense(fwd[...], cpl[k], NT)
        if k < 3:
            owned[k] = dense(sep[...], select(k))

    def select(k):
        level = LEVELS[k]
        start = lax.rem(ranks[k] * level.own, TILE)
        q = lax.broadcasted_iota(jnp.int32, (96, TILE), 0) - level.off
        lane = lax.broadcasted_iota(jnp.int32, (96, TILE), 1)
        hit = (q + start == lane) & (q >= 0) & (q < level.own)
        return jnp.where(hit, 1.0, 0.0)

    def tile_of(k):
        row = jnp.broadcast_to(lax.div(pos[k : k + 1, :], TILE), (8, TILE))
        tiles = LEVELS[k].tiles
        return jnp.broadcast_to(row[None], (tiles, 8, TILE)) == lax.broadcasted_iota(
            jnp.int32, (tiles, 8, TILE), 0
        )

    def own_tile(k):
        return lax.div(ranks[k] * LEVELS[k].own, TILE)

    def scatter(k, term, out):
        tiles = LEVELS[k].tiles
        hit = tile_of(k)
        high, lo = halves(-term)
        parts = [
            jnp.where(hit, jnp.broadcast_to(v[None], (tiles, 8, TILE)), 0.0).reshape(tiles * 8, TILE).astype(BF16)
            for v in (high, lo)
        ]
        out[...] = fast(jnp.concatenate(parts, axis=1), place[k]).reshape(tiles, 8, TILE)
        at = pl.ds(own_tile(k), 1)
        out[at] = out[at] + owned[k][None]

    def gather(k, full):
        tiles = LEVELS[k].tiles
        high, lo = halves(full[...].reshape(tiles * 8, TILE))
        got = fast(jnp.concatenate([high.astype(BF16), lo.astype(BF16)], axis=1), place_t[k])
        return jnp.sum(jnp.where(tile_of(k), got.reshape(tiles, 8, TILE), 0.0), axis=0)

    def remote(src, dst, slot, phase, target):
        return pltpu.make_async_remote_copy(
            src_ref=src, dst_ref=dst, send_sem=send_sem.at[slot, phase], recv_sem=recv_sem.at[slot, phase],
            device_id=target, device_id_type=MESH,
        )

    me = (a, c)
    leftover = []

    def total(k, slot, beside=None):
        level = LEVELS[k]
        w = level.share
        part, got, mine, seen, full = bufs[2 * k + slot]
        s = 2 * k + slot
        at = pl.ds(ordinal(level.scatter) * w, w)
        peers = masks_of(level.scatter)
        for n, mask in enumerate(peers):
            theirs = pl.ds(ordinal(level.scatter, mask) * w, w)
            remote(part.at[theirs], got.at[n], s, 0, device(mask)).start()
        if beside:
            beside()
        remote(got, got, s, 0, me).wait_recv()
        mine[...] = part[at] + jnp.sum(got[...], axis=0)
        for n, mask in enumerate(masks_of(level.exchange)):
            remote(mine, seen.at[n], s, 1, device(mask)).start()
        remote(seen, seen, s, 1, me).wait_recv()
        full[at] = mine[...] + jnp.sum(seen[...], axis=0)
        for mask in peers:
            remote(full.at[at], full.at[at], s, 2, device(mask)).start()
        others = full.at[pl.ds(0, level.tiles - w)]
        remote(others, others, s, 2, me).wait_recv()

        def finish():
            remote(others, others, s, 0, me).wait_send()
            remote(seen, seen, s, 1, me).wait_send()
            remote(got, got, s, 2, me).wait_send()

        leftover.append(finish)

    crowd = masks_of(SPARSE)
    n_crowd = len(crowd)
    early, terms, hots, owns, half, other, top = bufs[6]

    def introduce():
        owned_row = dense(sep[...], select(3))
        early[n_crowd, 0:8, :] = owned_row
        early[n_crowd, 8:9, :] = pos[3:4, :].astype(F32)
        for n, mask in enumerate(crowd):
            remote(early.at[n_crowd], early.at[n], 6, 0, device(mask)).start()

    def send_terms():
        terms[n_crowd] = -dense(fwd[...], cpl[3], NT)
        for n, mask in enumerate(crowd):
            remote(terms.at[n_crowd], terms.at[n], 6, 1, device(mask)).start()

    def meet():
        remote(early.at[pl.ds(0, n_crowd)], early.at[pl.ds(0, n_crowd)], 6, 0, me).wait_recv()
        owns[...] = jnp.zeros_like(owns)
        for n, mask in enumerate(crowd + [0]):
            at = pl.ds(ordinal((2, 4, 5, 6), mask), 1)
            owns[at] = owns[at] + early[n, 0:8, :][None]
        lanes = lax.broadcasted_iota(jnp.int32, (TILE, TILE), 0).astype(F32)

        def body(n, _):
            row = early[n, 8:9, :]
            lane = row - TILE * jnp.floor(row * (1.0 / TILE))
            hots[n] = jnp.where(jnp.broadcast_to(lane, (TILE, TILE)) == lanes, 1.0, 0.0).astype(BF16)
            return 0

        lax.fori_loop(0, n_crowd + 1, body, 0, unroll=4)

    def add_terms():
        remote(terms.at[pl.ds(0, n_crowd)], terms.at[pl.ds(0, n_crowd)], 6, 1, me).wait_recv()
        tiles = LEVELS[3].tiles
        counts = lax.broadcasted_iota(jnp.int32, (tiles, 8, TILE), 0).astype(F32)

        def one(n):
            tile = jnp.floor(early[n, 8:9, :] * (1.0 / TILE))
            hit = jnp.broadcast_to(tile[None], (tiles, 8, TILE)) == counts
            return jnp.concatenate(
                [
                    jnp.where(hit, jnp.broadcast_to(v[None], (tiles, 8, TILE)), 0.0).reshape(tiles * 8, TILE)
                    for v in halves(terms[n])
                ],
                axis=0,
            ).astype(BF16)

        def body(g, total):
            left = jnp.concatenate([one(2 * g), one(2 * g + 1)], axis=1)
            right = jnp.concatenate([hots[2 * g], hots[2 * g + 1]], axis=1)
            return total + fast(left, right, NT)

        both = lax.fori_loop(0, (n_crowd + 1) // 2, body, jnp.zeros((tiles * 16, TILE), F32), unroll=2)
        half[...] = owns[...] + (both[: tiles * 8] + both[tiles * 8 :]).reshape(tiles, 8, TILE)
        remote(half, other, 6, 2, device(1 << 4)).start()
        remote(other, other, 6, 2, me).wait_recv()
        top[...] = half[...] + other[...]

        def finish():
            remote(early.at[pl.ds(0, n_crowd)], early.at[pl.ds(0, n_crowd)], 6, 0, me).wait_send()
            remote(terms.at[pl.ds(0, n_crowd)], terms.at[pl.ds(0, n_crowd)], 6, 1, me).wait_send()
            remote(half, half, 6, 2, me).wait_send()

        leftover.append(finish)

    def times_rows(k, full):
        factor = factors[k]
        m = LEVELS[k].own

        def body(j, sums):
            tile = full[j]
            rows = factor[:, pl.ds(pl.multiple_of(j * TILE, TILE), TILE)]
            return tuple(sums[q] + tile * rows[q : q + 1, :] for q in range(m))

        sums = lax.fori_loop(0, LEVELS[k].tiles, body, tuple(jnp.zeros((8, TILE), F32) for _ in range(m)), unroll=4)
        return [jnp.sum(v, axis=1, keepdims=True) for v in sums]

    def spread(k, values, out):
        factor = factors[k]
        m = LEVELS[k].own
        wide = [jnp.broadcast_to(v, (8, TILE)) for v in values]

        def body(j, _):
            rows = factor[:, pl.ds(pl.multiple_of(j * TILE, TILE), TILE)]
            acc = wide[0] * rows[0:1, :]
            for q in range(1, m):
                acc = acc + wide[q] * rows[q : q + 1, :]
            out[j] = acc
            return 0

        lax.fori_loop(0, LEVELS[k].tiles, body, 0, unroll=4)

    def inverse_blocks():
        vmat[...] = jnp.zeros_like(vmat)
        for j in range(4):
            vmat[j * TILE : (j + 1) * TILE, j * TILE : (j + 1) * TILE] = inv[j]
        for j in (2, 1, 0):
            step = -dense(inv[j], sub[j])
            vmat[j * TILE : (j + 1) * TILE, (j + 1) * TILE :] = dense(
                step, vmat[(j + 1) * TILE : (j + 2) * TILE, (j + 1) * TILE :]
            )

    def coupled():
        cv[...] = dense(cpl[3], vmat[...], NT)

    copies[0].wait()
    copies[1].wait()
    pl.semaphore_wait(barrier, len(greet))
    introduce()

    for n in range(2, 5):
        copies[n].wait()
    earlier = None
    for j in range(4):
        current = rhs[:, j * TILE : (j + 1) * TILE]
        if j:
            current = current - dense(earlier, sub[j - 1])
        earlier = dense(current, inv[j])
        fwd[:, j * TILE : (j + 1) * TILE] = earlier
    copies[5].wait()
    send_terms()
    meet()
    copies[6].wait()
    prepare(2)
    copies[7].wait()
    copies[8].wait()
    add_terms()

    def beside_three():
        prepare(1)
        prepare(0)
        prepare(3)
        inverse_blocks()

    besides = {2: beside_three, 1: coupled}
    for k in (3, 2, 1, 0):
        m = LEVELS[k].own
        if k < 3:
            total(k, 0, besides.get(k))
            copies[{2: 9, 1: 11, 0: 13}[k]].wait()
            if k:
                copies[{2: 10, 1: 12}[k]].wait()
        values = times_rows(k, bufs[2 * k][4] if k < 3 else top)
        if k:
            term = base[k - 1]
            for q in range(m):
                term = term + values[q] * links[k - 1][q : q + 1, :]
            scatter(k - 1, term, bufs[2 * (k - 1)][0])
            for q in range(m):
                zval[LEVELS[k].off + q] = jnp.broadcast_to(values[q], (8, TILE))

    picked = None
    for k in range(4):
        m = LEVELS[k].own
        if k:
            values = [
                zval[LEVELS[k].off + q]
                - jnp.sum(picked * links[k - 1][q : q + 1, :], axis=1, keepdims=True)
                for q in range(m)
            ]
        spread(k, values, bufs[2 * k + 1][0])

        def after(k=k, picked=picked):
            if k == 0:
                work[...] = fwd[...]
                sep_out[...] = jnp.zeros_like(sep_out)
                return
            work[...] = work[...] - dense(picked, cpl[k - 1])
            sep_out[...] = sep_out[...] + dense(bufs[2 * k - 1][4][pl.ds(own_tile(k - 1), 1)][0], select(k - 1), NT)
            if k == 3:
                work[...] = dense(work[...], vmat[...], NT)

        total(k, 1, after)
        picked = gather(k, bufs[2 * k + 1][4])
    leaf_out[...] = work[...] - dense(picked, cv[...])
    sep_out[...] = sep_out[...] + dense(bufs[7][4][pl.ds(own_tile(3), 1)][0], select(3), NT)
    for finish in leftover:
        finish()


def local(*args):
    ins = [x[0, 0] for x in args]
    order = ins
    vmem = [pltpu.VMEM(x.shape, x.dtype) for x in order]
    bufs = []
    for k, level in enumerate(LEVELS):
        w = level.share
        n_crowd = 1 << len(SPARSE)
        shapes = (
            (level.tiles, 8, TILE),
            ((1 << len(level.scatter)) - 1, w, 8, TILE),
            (w, 8, TILE),
            ((1 << len(level.exchange)) - 1, w, 8, TILE),
            (level.tiles, 8, TILE),
        )
        usual = tuple(pltpu.VMEM(s, F32) for s in shapes)
        whole = pltpu.VMEM((level.tiles, 8, TILE), F32)
        if k == 3:
            bufs.append(
                (
                    pltpu.VMEM((n_crowd, 9, TILE), F32),
                    pltpu.VMEM((n_crowd, 8, TILE), F32),
                    pltpu.VMEM((n_crowd, TILE, TILE), BF16),
                    whole,
                    whole,
                    whole,
                    whole,
                )
            )
        else:
            bufs.append(usual)
        bufs.append(usual)
    scratch = vmem + [
        pltpu.VMEM((8, 512), F32),
        pltpu.VMEM((4, 8, TILE), F32),
        pltpu.VMEM((4, 2 * TILE, TILE), BF16),
        pltpu.VMEM((4, 2 * TILE, TILE), BF16),
        pltpu.VMEM((4, 8, TILE), F32),
        pltpu.VMEM((96, 8, TILE), F32),
        pltpu.VMEM((512, 512), F32),
        pltpu.VMEM((TILE, 512), F32),
        pltpu.VMEM((8, 512), F32),
    ]
    sems = (
        pltpu.SemaphoreType.DMA((14,)),
        pltpu.SemaphoreType.DMA((8, 3)),
        pltpu.SemaphoreType.DMA((8, 3)),
    )
    leaf, sep = pl.pallas_call(
        kernel,
        out_shape=(jax.ShapeDtypeStruct((8, 512), F32), jax.ShapeDtypeStruct((8, 96), F32)),
        in_specs=[pl.BlockSpec(memory_space=pltpu.HBM)] * len(ins),
        out_specs=(pl.BlockSpec(memory_space=pltpu.VMEM),) * 2,
        scratch_shapes=scratch + bufs + [sems],
        compiler_params=pltpu.CompilerParams(
            collective_id=0, has_side_effects=True, vmem_limit_bytes=60 * 1024 * 1024
        ),
        name="nested_solve",
    )(*ins)
    return leaf[None, None], sep[None, None]


def solution(mesh):
    four = P("gx", "gy", None, None)
    five = P("gx", "gy", None, None, None)
    in_specs = (four, five, five, four, four, five) + (four,) * 7
    return jax.shard_map(local, mesh=mesh, in_specs=in_specs, out_specs=(four, four), check_vma=False)
```

```python
import functools

import jax
import jax.numpy as jnp
from jax import lax
from jax.experimental import pallas as pl
from jax.experimental.pallas import tpu as pltpu
from jax.sharding import PartitionSpec as P

MESH = pl.DeviceIdType.MESH
F32 = jnp.float32
BF16 = jnp.bfloat16
HIGHEST = lax.Precision.HIGHEST
NN = (((1,), (0,)), ((), ()))
NT = (((1,), (1,)), ((), ()))
TILE = 128
NX, NY, NC, NZ = 4, 4, 2, 16


def dense(a, b, dims=NN):
    return lax.dot_general(a, b, dims, precision=HIGHEST, preferred_element_type=F32)


def fast(a, b, dims=NN):
    return lax.dot_general(a, b, dims, preferred_element_type=F32)


def halves(v):
    high = v.astype(BF16).astype(F32)
    return high, v - high


class Level:
    def __init__(self, own, width, off, scatter, exchange):
        self.own = own
        self.width = width
        self.tiles = width // TILE
        self.off = off
        self.scatter = scatter
        self.exchange = exchange
        self.share = self.tiles >> len(scatter)


LEVELS = (
    Level(16, 8192, 0, (0, 1, 2, 3, 4, 5), (6, 7, 8)),
    Level(16, 4096, 16, (0, 1, 2, 3, 4), (5, 6, 7)),
    Level(32, 4096, 32, (0, 1, 2, 4), (5, 6, 7)),
    Level(32, 2048, 64, (0, 1, 4), (2, 5, 6)),
)
SPARSE = (0, 1, 2, 5, 6)
CORE = (4,)
MID_SCATTER = (4,)
MID_EXCHANGES = ((0, 1, 5), (2, 3))


def hops(mask):
    def ring(n, m):
        return max(min(abs(v - (v ^ m)), n - abs(v - (v ^ m))) for v in range(n))

    return ring(4, mask & 3) + ring(4, mask >> 2 & 3) + ring(16, mask >> 5) + 0.1 * (mask >> 4 & 1)


def masks_of(bits):
    out = [0]
    for b in bits:
        out = out + [m | 1 << b for m in out]
    return sorted(out[1:], key=lambda m: (-hops(m), m))


def kernel(
    rhs_h, inv_h, sub_h, sep_h, pos_h, cpl_h, f1_h, f2_h, f3_h, f4_h, l2_h, l3_h, l4_h,
    leaf_out, sep_out,
    rhs, inv, sub, sep, pos, cpl, f2, f3, f4, l2, l3, l4,
    fwd, base, place_t, place, owned, zval, vmat, cv, work, cols,
    *rest,
):
    bufs = rest[:8]
    mids = rest[8]
    in_sem, send_sem, recv_sem = rest[9]
    factors = (None, f2, f3, f4)
    links = (l2, l3, l4)

    a, c = lax.axis_index("gx"), lax.axis_index("gy")
    index = a * 16 + c
    bit = [lax.rem(lax.div(index, 1 << j), 2) for j in range(9)]
    flip = [1 - 2 * v for v in bit]

    def device(mask):
        x, y = a, c
        for j in range(9):
            if mask >> j & 1:
                if j < 4:
                    y = y + flip[j] * (1 << j)
                else:
                    x = x + flip[j] * (1 << (j - 4))
        return (x, y)

    def ordinal(bits, mask=0):
        r = 0
        for n, j in enumerate(bits):
            r = r + bit[j] * (1 << n)
            if mask >> j & 1:
                r = r + flip[j] * (1 << n)
        return r

    low = lax.rem(index, 256)
    ranks = (
        index,
        low,
        lax.div(low, 16) * 8 + lax.rem(index, 8),
        lax.div(lax.rem(index, 128), 16) * 8 + lax.rem(index, 8),
    )

    pairs = (
        (sep_h, sep), (pos_h, pos), (rhs_h, rhs), (inv_h, inv), (sub_h, sub),
        (cpl_h.at[3], cpl.at[3]), (cpl_h.at[pl.ds(0, 3)], cpl.at[pl.ds(0, 3)]),
        (f4_h, f4), (l4_h, l4), (f3_h, f3), (l3_h, l3), (f2_h, f2), (l2_h, l2),
    )
    copies = [pltpu.make_async_copy(s, d, in_sem.at[n]) for n, (s, d) in enumerate(pairs)]
    for copy in copies:
        copy.start()

    barrier = pltpu.get_barrier_semaphore()
    greet = set(masks_of(SPARSE)) | set(masks_of(CORE))
    for level in LEVELS:
        greet |= set(masks_of(level.scatter)) | set(masks_of(level.exchange))
    for mask in sorted(greet, key=lambda m: (-hops(m), m)):
        pl.semaphore_signal(barrier, inc=1, device_id=device(mask), device_id_type=MESH)

    def prepare(k):
        level = LEVELS[k]
        row = pos[k : k + 1, :]
        lane = lax.rem(row, TILE)
        hot = jnp.broadcast_to(lane, (TILE, TILE)) == lax.broadcasted_iota(jnp.int32, (TILE, TILE), 0)
        hot = jnp.where(hot, 1.0, 0.0)
        turned = jnp.transpose(hot).astype(BF16)
        hot = hot.astype(BF16)
        place_t[k] = jnp.concatenate([hot, hot], axis=0)
        place[k] = jnp.concatenate([turned, turned], axis=0)
        if k < 3:
            base[k] = dense(fwd[...], cpl[k], NT)
        if k < 3:
            owned[k] = dense(sep[...], select(k))

    def select(k):
        level = LEVELS[k]
        start = lax.rem(ranks[k] * level.own, TILE)
        q = lax.broadcasted_iota(jnp.int32, (96, TILE), 0) - level.off
        lane = lax.broadcasted_iota(jnp.int32, (96, TILE), 1)
        hit = (q + start == lane) & (q >= 0) & (q < level.own)
        return jnp.where(hit, 1.0, 0.0)

    def tile_of(k):
        row = jnp.broadcast_to(lax.div(pos[k : k + 1, :], TILE), (8, TILE))
        tiles = LEVELS[k].tiles
        return jnp.broadcast_to(row[None], (tiles, 8, TILE)) == lax.broadcasted_iota(
            jnp.int32, (tiles, 8, TILE), 0
        )

    def own_tile(k):
        return lax.div(ranks[k] * LEVELS[k].own, TILE)

    def scatter(k, term, out):
        tiles = LEVELS[k].tiles
        hit = tile_of(k)
        high, lo = halves(-term)
        parts = [
            jnp.where(hit, jnp.broadcast_to(v[None], (tiles, 8, TILE)), 0.0).reshape(tiles * 8, TILE).astype(BF16)
            for v in (high, lo)
        ]
        out[...] = fast(jnp.concatenate(parts, axis=1), place[k]).reshape(tiles, 8, TILE)
        at = pl.ds(own_tile(k), 1)
        out[at] = out[at] + owned[k][None]

    def gather(k, full):
        tiles = LEVELS[k].tiles
        high, lo = halves(full[...].reshape(tiles * 8, TILE))
        got = fast(jnp.concatenate([high.astype(BF16), lo.astype(BF16)], axis=1), place_t[k])
        return jnp.sum(jnp.where(tile_of(k), got.reshape(tiles, 8, TILE), 0.0), axis=0)

    def remote(src, dst, sem, target):
        return pltpu.make_async_remote_copy(
            src_ref=src, dst_ref=dst, send_sem=send_sem.at[sem], recv_sem=recv_sem.at[sem],
            device_id=target, device_id_type=MESH,
        )

    me = (a, c)
    leftover = []

    def finish(ref, sem):
        leftover.append(lambda: remote(ref, ref, sem, me).wait_send())

    def arrive(ref, sem):
        remote(ref, ref, sem, me).wait_recv()

    def send_shares(part, got, bits, w, sem):
        for n, mask in enumerate(masks_of(bits)):
            theirs = pl.ds(ordinal(bits, mask) * w, w)
            remote(part.at[theirs], got.at[n], sem, device(mask)).start()
        finish(got, sem)

    def send_all(ref, seen, bits, sem):
        for n, mask in enumerate(masks_of(bits)):
            remote(ref, seen.at[n], sem, device(mask)).start()
        finish(seen, sem)

    def send_mine(full, bits, w, sem):
        at = pl.ds(ordinal(bits) * w, w)
        for mask in masks_of(bits):
            remote(full.at[at], full.at[at], sem, device(mask)).start()
        finish(full.at[pl.ds(0, full.shape[0] - w)], sem)

    def combine(k, slot, beside=None, spare=None):
        level = LEVELS[k]
        w = level.share
        part, got, mine, seen = bufs[2 * k + slot][:4]
        s = 3 * (2 * k + slot)
        if not slot:
            send_shares(part, got, level.scatter, w, s)
        if beside:
            beside()
        arrive(got, s)
        mine[...] = part[pl.ds(ordinal(level.scatter) * w, w)] + jnp.sum(got[...], axis=0)
        return swap(k, slot, spare)

    def swap(k, slot, spare=None):
        mine, seen = bufs[2 * k + slot][2:4]
        s = 3 * (2 * k + slot) + 1
        send_all(mine, seen, LEVELS[k].exchange, s)
        if spare:
            spare()
        arrive(seen, s)
        return mine[...] + jnp.sum(seen[...], axis=0)

    def spread_out(k, slot, value):
        level = LEVELS[k]
        w = level.share
        full = bufs[2 * k + slot][4]
        s = 3 * (2 * k + slot) + 2
        full[pl.ds(ordinal(level.scatter) * w, w)] = value
        send_mine(full, level.scatter, w, s)
        arrive(full.at[pl.ds(0, level.tiles - w)], s)

    top_bits = LEVELS[0].scatter
    n_top = 1 << len(top_bits)

    def columns(mask=0):
        return pl.ds(pl.multiple_of(ordinal(top_bits, mask) * TILE, TILE), TILE)

    def send_columns():
        mine = cols.at[ordinal(top_bits)]
        pltpu.make_async_copy(f1_h.at[:, columns()], mine, in_sem.at[13]).start()
        for mask in masks_of(top_bits):
            remote(f1_h.at[:, columns(mask)], mine, 24, device(mask)).start()
        finish(cols.at[pl.ds(0, n_top - 1)], 24)

    def columns_here():
        pltpu.make_async_copy(f1_h.at[:, columns()], cols.at[ordinal(top_bits)], in_sem.at[13]).wait()
        arrive(cols.at[pl.ds(0, n_top - 1)], 24)

    def middle(tile):
        rows = n_top * LEVELS[0].own
        part = dense(tile, cols[...].reshape(rows, TILE), NT)
        zbuf, zgot, zmine, zseen, znext, zlast, zfull = mids
        n = rows // TILE
        for j in range(n):
            zbuf[j] = part[:, j * TILE : (j + 1) * TILE]
        w = n >> len(MID_SCATTER)
        at = pl.ds(ordinal(MID_SCATTER) * w, w)
        send_shares(zbuf, zgot, MID_SCATTER, w, 25)
        arrive(zgot, 25)
        zmine[...] = zbuf[at] + jnp.sum(zgot[...], axis=0)
        send_all(zmine, zseen, MID_EXCHANGES[0], 26)
        arrive(zseen, 26)
        znext[...] = zmine[...] + jnp.sum(zseen[...], axis=0)
        send_all(znext, zlast, MID_EXCHANGES[1], 28)
        arrive(zlast, 28)
        zfull[at] = znext[...] + jnp.sum(zlast[...], axis=0)
        send_mine(zfull, MID_SCATTER, w, 27)
        arrive(zfull.at[pl.ds(0, n - w)], 27)
        whole = jnp.concatenate([zfull[j] for j in range(n)], axis=1)
        return dense(whole, cols[...].reshape(rows, TILE))

    crowd = masks_of(SPARSE)
    n_crowd = len(crowd)
    early, terms, hots, owns, half, other, top = bufs[6]

    def introduce():
        for n, mask in enumerate(crowd):
            remote(early.at[n_crowd], early.at[n], 18, device(mask)).start()
        finish(early.at[pl.ds(0, n_crowd)], 18)

    def send_terms():
        terms[n_crowd] = -dense(fwd[...], cpl[3], NT)
        for n, mask in enumerate(crowd):
            remote(terms.at[n_crowd], terms.at[n], 19, device(mask)).start()
        finish(terms.at[pl.ds(0, n_crowd)], 19)

    def meet():
        arrive(early.at[pl.ds(0, n_crowd)], 18)
        owns[...] = jnp.zeros_like(owns)
        for n, mask in enumerate(crowd + [0]):
            at = pl.ds(ordinal((2, 4, 5, 6), mask), 1)
            owns[at] = owns[at] + early[n, 0:8, :][None]
        lanes = lax.broadcasted_iota(jnp.int32, (TILE, TILE), 0).astype(F32)

        def body(n, _):
            row = early[n, 8:9, :]
            lane = row - TILE * jnp.floor(row * (1.0 / TILE))
            hots[n] = jnp.where(jnp.broadcast_to(lane, (TILE, TILE)) == lanes, 1.0, 0.0).astype(BF16)
            return 0

        lax.fori_loop(0, n_crowd + 1, body, 0, unroll=4)

    def add_terms():
        arrive(terms.at[pl.ds(0, n_crowd)], 19)
        tiles = LEVELS[3].tiles
        counts = lax.broadcasted_iota(jnp.int32, (tiles, 8, TILE), 0).astype(F32)

        def one(n):
            tile = jnp.floor(early[n, 8:9, :] * (1.0 / TILE))
            hit = jnp.broadcast_to(tile[None], (tiles, 8, TILE)) == counts
            return jnp.concatenate(
                [
                    jnp.where(hit, jnp.broadcast_to(v[None], (tiles, 8, TILE)), 0.0).reshape(tiles * 8, TILE)
                    for v in halves(terms[n])
                ],
                axis=0,
            ).astype(BF16)

        def body(g, total):
            left = jnp.concatenate([one(2 * g), one(2 * g + 1)], axis=1)
            right = jnp.concatenate([hots[2 * g], hots[2 * g + 1]], axis=1)
            return total + fast(left, right, NT)

        both = lax.fori_loop(0, (n_crowd + 1) // 2, body, jnp.zeros((tiles * 16, TILE), F32), unroll=2)
        half[...] = owns[...] + (both[: tiles * 8] + both[tiles * 8 :]).reshape(tiles, 8, TILE)
        remote(half, other, 20, device(1 << 4)).start()
        finish(half, 20)
        arrive(other, 20)
        top[...] = half[...] + other[...]

    def times_rows(k, full):
        factor = factors[k]
        m = LEVELS[k].own

        def body(j, sums):
            tile = full[j]
            rows = factor[:, pl.ds(pl.multiple_of(j * TILE, TILE), TILE)]
            return tuple(sums[q] + tile * rows[q : q + 1, :] for q in range(m))

        sums = lax.fori_loop(0, LEVELS[k].tiles, body, tuple(jnp.zeros((8, TILE), F32) for _ in range(m)), unroll=4)
        return [jnp.sum(v, axis=1, keepdims=True) for v in sums]

    def spread_share(k, wide, out, place):
        factor = factors[k]
        w = LEVELS[k].share
        for j in range(w):
            tile = place * w + j
            rows = factor[:, pl.ds(pl.multiple_of(tile * TILE, TILE), TILE)]
            acc = wide[0] * rows[0:1, :]
            for q in range(1, LEVELS[k].own):
                acc = acc + wide[q] * rows[q : q + 1, :]
            out[tile] = acc

    def spread_send(k, values):
        part, got = bufs[2 * k + 1][:2]
        bits = LEVELS[k].scatter
        w = LEVELS[k].share
        s = 3 * (2 * k + 1)
        wide = [jnp.broadcast_to(v, (8, TILE)) for v in values]
        for n, mask in enumerate(masks_of(bits)):
            place = ordinal(bits, mask)
            spread_share(k, wide, part, place)
            remote(part.at[pl.ds(place * w, w)], got.at[n], s, device(mask)).start()
        spread_share(k, wide, part, ordinal(bits))
        finish(got, s)

    def spread(k, values, out):
        factor = factors[k]
        m = LEVELS[k].own
        wide = [jnp.broadcast_to(v, (8, TILE)) for v in values]

        def body(j, _):
            rows = factor[:, pl.ds(pl.multiple_of(j * TILE, TILE), TILE)]
            acc = wide[0] * rows[0:1, :]
            for q in range(1, m):
                acc = acc + wide[q] * rows[q : q + 1, :]
            out[j] = acc
            return 0

        lax.fori_loop(0, LEVELS[k].tiles, body, 0, unroll=4)

    def inverse_blocks():
        vmat[...] = jnp.zeros_like(vmat)
        for j in range(4):
            vmat[j * TILE : (j + 1) * TILE, j * TILE : (j + 1) * TILE] = inv[j]
        for j in (2, 1, 0):
            step = -dense(inv[j], sub[j])
            vmat[j * TILE : (j + 1) * TILE, (j + 1) * TILE :] = dense(
                step, vmat[(j + 1) * TILE : (j + 2) * TILE, (j + 1) * TILE :]
            )

    def coupled():
        cv[...] = dense(cpl[3], vmat[...], NT)

    for n in range(6):
        copies[n].wait()
    early[n_crowd, 0:8, :] = dense(sep[...], select(3))
    early[n_crowd, 8:9, :] = pos[3:4, :].astype(F32)
    pl.semaphore_wait(barrier, len(greet))
    introduce()

    earlier = None
    for j in range(4):
        current = rhs[:, j * TILE : (j + 1) * TILE]
        if j:
            current = current - dense(earlier, sub[j - 1])
        earlier = dense(current, inv[j])
        fwd[:, j * TILE : (j + 1) * TILE] = earlier
    send_terms()
    meet()
    copies[6].wait()
    prepare(2)
    copies[7].wait()
    copies[8].wait()
    add_terms()

    def beside_three():
        prepare(1)
        prepare(0)
        prepare(3)
        inverse_blocks()

    values = None
    for k in (3, 2, 1, 0):
        m = LEVELS[k].own
        full = top
        if k == 2:
            value = combine(2, 0, beside_three)
        elif k == 1:
            value = combine(1, 0, coupled, send_columns)
        elif k == 0:
            bufs[1][2][...] = middle(combine(0, 0, columns_here)[0])[None]
            break
        if k < 3:
            spread_out(k, 0, value)
            full = bufs[2 * k][4]
            copies[{2: 9, 1: 11}[k]].wait()
            copies[{2: 10, 1: 12}[k]].wait()
        values = times_rows(k, full)
        term = base[k - 1]
        for q in range(m):
            term = term + values[q] * links[k - 1][q : q + 1, :]
        scatter(k - 1, term, bufs[2 * (k - 1)][0])
        for q in range(m):
            zval[LEVELS[k].off + q] = jnp.broadcast_to(values[q], (8, TILE))

    picked = None
    for k in range(4):
        m = LEVELS[k].own
        if k:
            values = [
                zval[LEVELS[k].off + q]
                - jnp.sum(picked * links[k - 1][q : q + 1, :], axis=1, keepdims=True)
                for q in range(m)
            ]
            spread_send(k, values)

        def after(k=k, picked=picked):
            if k == 0:
                work[...] = fwd[...]
                sep_out[...] = jnp.zeros_like(sep_out)
                return
            work[...] = work[...] - dense(picked, cpl[k - 1])
            sep_out[...] = sep_out[...] + dense(bufs[2 * k - 1][4][pl.ds(own_tile(k - 1), 1)][0], select(k - 1), NT)
            if k == 3:
                work[...] = dense(work[...], vmat[...], NT)

        value = combine(k, 1, after) if k else swap(0, 1, after)
        spread_out(k, 1, value)
        picked = gather(k, bufs[2 * k + 1][4])
    leaf_out[...] = work[...] - dense(picked, cv[...])
    sep_out[...] = sep_out[...] + dense(bufs[7][4][pl.ds(own_tile(3), 1)][0], select(3), NT)
    for sent in leftover:
        sent()


def local(*args):
    ins = [x[0, 0] for x in args]
    vmem = [pltpu.VMEM(x.shape, x.dtype) for n, x in enumerate(ins) if n != 6]
    bufs = []
    for k, level in enumerate(LEVELS):
        w = level.share
        n_crowd = 1 << len(SPARSE)
        shapes = (
            (level.tiles, 8, TILE),
            ((1 << len(level.scatter)) - 1, w, 8, TILE),
            (w, 8, TILE),
            ((1 << len(level.exchange)) - 1, w, 8, TILE),
            (level.tiles, 8, TILE),
        )
        usual = tuple(pltpu.VMEM(s, F32) for s in shapes)
        whole = pltpu.VMEM((level.tiles, 8, TILE), F32)
        if k == 3:
            bufs.append(
                (
                    pltpu.VMEM((n_crowd, 9, TILE), F32),
                    pltpu.VMEM((n_crowd, 8, TILE), F32),
                    pltpu.VMEM((n_crowd, TILE, TILE), BF16),
                    whole,
                    whole,
                    whole,
                    whole,
                )
            )
        else:
            bufs.append(usual)
        bufs.append(usual)
    scratch = vmem + [
        pltpu.VMEM((8, 512), F32),
        pltpu.VMEM((4, 8, TILE), F32),
        pltpu.VMEM((4, 2 * TILE, TILE), BF16),
        pltpu.VMEM((4, 2 * TILE, TILE), BF16),
        pltpu.VMEM((4, 8, TILE), F32),
        pltpu.VMEM((96, 8, TILE), F32),
        pltpu.VMEM((512, 512), F32),
        pltpu.VMEM((TILE, 512), F32),
        pltpu.VMEM((8, 512), F32),
        pltpu.VMEM((1 << len(LEVELS[0].scatter), LEVELS[0].own, TILE), F32),
    ]
    n = (LEVELS[0].own << len(LEVELS[0].scatter)) // TILE
    w = n >> len(MID_SCATTER)
    mids = tuple(
        pltpu.VMEM(s + (8, TILE), F32)
        for s in (
            (n,),
            ((1 << len(MID_SCATTER)) - 1, w),
            (w,),
            ((1 << len(MID_EXCHANGES[0])) - 1, w),
            (w,),
            ((1 << len(MID_EXCHANGES[1])) - 1, w),
            (n,),
        )
    )
    sems = (
        pltpu.SemaphoreType.DMA((14,)),
        pltpu.SemaphoreType.DMA((32,)),
        pltpu.SemaphoreType.DMA((32,)),
    )
    leaf, sep = pl.pallas_call(
        kernel,
        out_shape=(jax.ShapeDtypeStruct((8, 512), F32), jax.ShapeDtypeStruct((8, 96), F32)),
        in_specs=[pl.BlockSpec(memory_space=pltpu.HBM)] * len(ins),
        out_specs=(pl.BlockSpec(memory_space=pltpu.VMEM),) * 2,
        scratch_shapes=scratch + bufs + [mids, sems],
        compiler_params=pltpu.CompilerParams(
            collective_id=0, has_side_effects=True, vmem_limit_bytes=60 * 1024 * 1024
        ),
        name="nested_solve",
    )(*ins)
    return leaf[None, None], sep[None, None]


def solution(mesh):
    four = P("gx", "gy", None, None)
    five = P("gx", "gy", None, None, None)
    in_specs = (four, five, five, four, four, five) + (four,) * 7
    return jax.shard_map(local, mesh=mesh, in_specs=in_specs, out_specs=(four, four), check_vma=False)
```

```python
import functools

import jax
import jax.numpy as jnp
from jax import lax
from jax.experimental import pallas as pl
from jax.experimental.pallas import tpu as pltpu
from jax.sharding import PartitionSpec as P

MESH = pl.DeviceIdType.MESH
F32 = jnp.float32
BF16 = jnp.bfloat16
HIGHEST = lax.Precision.HIGHEST
NN = (((1,), (0,)), ((), ()))
NT = (((1,), (1,)), ((), ()))
TILE = 128
NX, NY, NC, NZ = 4, 4, 2, 16


def dense(a, b, dims=NN):
    return lax.dot_general(a, b, dims, precision=HIGHEST, preferred_element_type=F32)


def fast(a, b, dims=NN):
    return lax.dot_general(a, b, dims, preferred_element_type=F32)


def halves(v):
    high = v.astype(BF16).astype(F32)
    return high, v - high


class Level:
    def __init__(self, own, width, off, scatter, exchange):
        self.own = own
        self.width = width
        self.tiles = width // TILE
        self.off = off
        self.scatter = scatter
        self.exchange = exchange
        self.share = self.tiles >> len(scatter)


LEVELS = (
    Level(16, 8192, 0, (0, 1, 2, 3, 4, 5), (6, 7, 8)),
    Level(16, 4096, 16, (0, 1, 2, 3, 4), (5, 6, 7)),
    Level(32, 4096, 32, (0, 1, 2, 4), (5, 6, 7)),
    Level(32, 2048, 64, (0, 1, 4), (2, 5, 6)),
)
SPARSE = (0, 1, 2, 5, 6)
CORE = (4,)
MID_SCATTER = (4,)
MID_EXCHANGES = ((0, 1, 5), (2, 3))


def hops(mask):
    def ring(n, m):
        return max(min(abs(v - (v ^ m)), n - abs(v - (v ^ m))) for v in range(n))

    return ring(4, mask & 3) + ring(4, mask >> 2 & 3) + ring(16, mask >> 5) + 0.1 * (mask >> 4 & 1)


def masks_of(bits):
    out = [0]
    for b in bits:
        out = out + [m | 1 << b for m in out]
    return sorted(out[1:], key=lambda m: (-hops(m), m))


def kernel(
    rhs_h, inv_h, sub_h, sep_h, pos_h, cpl_h, f1_h, f2_h, f3_h, f4_h, l2_h, l3_h, l4_h,
    leaf_out, sep_out,
    rhs, inv, sub, sep, pos, cpl, f2, f3, f4, l2, l3, l4,
    fwd, base, place_t, place, owned, zval, vmat, cv, work, cols,
    *rest,
):
    bufs = rest[:8]
    mids = rest[8]
    in_sem, send_sem, recv_sem = rest[9]
    factors = (None, f2, f3, f4)
    links = (l2, l3, l4)

    a, c = lax.axis_index("gx"), lax.axis_index("gy")
    index = a * 16 + c
    bit = [lax.rem(lax.div(index, 1 << j), 2) for j in range(9)]
    flip = [1 - 2 * v for v in bit]

    def device(mask):
        x, y = a, c
        for j in range(9):
            if mask >> j & 1:
                if j < 4:
                    y = y + flip[j] * (1 << j)
                else:
                    x = x + flip[j] * (1 << (j - 4))
        return (x, y)

    def ordinal(bits, mask=0):
        r = 0
        for n, j in enumerate(bits):
            r = r + bit[j] * (1 << n)
            if mask >> j & 1:
                r = r + flip[j] * (1 << n)
        return r

    low = lax.rem(index, 256)
    ranks = (
        index,
        low,
        lax.div(low, 16) * 8 + lax.rem(index, 8),
        lax.div(lax.rem(index, 128), 16) * 8 + lax.rem(index, 8),
    )

    pairs = (
        (sep_h, sep), (pos_h, pos), (rhs_h, rhs), (inv_h, inv), (sub_h, sub),
        (cpl_h.at[3], cpl.at[3]), (cpl_h.at[pl.ds(0, 3)], cpl.at[pl.ds(0, 3)]),
        (f4_h, f4), (l4_h, l4), (f3_h, f3), (l3_h, l3), (f2_h, f2), (l2_h, l2),
    )
    copies = [pltpu.make_async_copy(s, d, in_sem.at[n]) for n, (s, d) in enumerate(pairs)]
    for copy in copies:
        copy.start()

    barrier = pltpu.get_barrier_semaphore()
    greet = set(masks_of(SPARSE)) | set(masks_of(CORE))
    for level in LEVELS:
        greet |= set(masks_of(level.scatter)) | set(masks_of(level.exchange))
    for mask in sorted(greet, key=lambda m: (-hops(m), m)):
        pl.semaphore_signal(barrier, inc=1, device_id=device(mask), device_id_type=MESH)

    def prepare(k):
        level = LEVELS[k]
        row = pos[k : k + 1, :]
        lane = lax.rem(row, TILE)
        hot = jnp.broadcast_to(lane, (TILE, TILE)) == lax.broadcasted_iota(jnp.int32, (TILE, TILE), 0)
        hot = jnp.where(hot, 1.0, 0.0)
        turned = jnp.transpose(hot).astype(BF16)
        hot = hot.astype(BF16)
        place_t[k] = jnp.concatenate([hot, hot], axis=0)
        place[k] = jnp.concatenate([turned, turned], axis=0)
        if k < 3:
            base[k] = dense(fwd[...], cpl[k], NT)
        if k < 3:
            owned[k] = dense(sep[...], select(k))

    def select(k):
        level = LEVELS[k]
        start = lax.rem(ranks[k] * level.own, TILE)
        q = lax.broadcasted_iota(jnp.int32, (96, TILE), 0) - level.off
        lane = lax.broadcasted_iota(jnp.int32, (96, TILE), 1)
        hit = (q + start == lane) & (q >= 0) & (q < level.own)
        return jnp.where(hit, 1.0, 0.0)

    def tile_of(k):
        row = jnp.broadcast_to(lax.div(pos[k : k + 1, :], TILE), (8, TILE))
        tiles = LEVELS[k].tiles
        return jnp.broadcast_to(row[None], (tiles, 8, TILE)) == lax.broadcasted_iota(
            jnp.int32, (tiles, 8, TILE), 0
        )

    def own_tile(k):
        return lax.div(ranks[k] * LEVELS[k].own, TILE)

    def scatter(k, term, out):
        tiles = LEVELS[k].tiles
        hit = tile_of(k)
        high, lo = halves(-term)
        parts = [
            jnp.where(hit, jnp.broadcast_to(v[None], (tiles, 8, TILE)), 0.0).reshape(tiles * 8, TILE).astype(BF16)
            for v in (high, lo)
        ]
        out[...] = fast(jnp.concatenate(parts, axis=1), place[k]).reshape(tiles, 8, TILE)
        at = pl.ds(own_tile(k), 1)
        out[at] = out[at] + owned[k][None]

    def gather(k, full):
        tiles = LEVELS[k].tiles
        high, lo = halves(full[...].reshape(tiles * 8, TILE))
        got = fast(jnp.concatenate([high.astype(BF16), lo.astype(BF16)], axis=1), place_t[k])
        return jnp.sum(jnp.where(tile_of(k), got.reshape(tiles, 8, TILE), 0.0), axis=0)

    def remote(src, dst, sem, target):
        return pltpu.make_async_remote_copy(
            src_ref=src, dst_ref=dst, send_sem=send_sem.at[sem], recv_sem=recv_sem.at[sem],
            device_id=target, device_id_type=MESH,
        )

    me = (a, c)
    leftover = []

    def finish(ref, sem):
        leftover.append(lambda: remote(ref, ref, sem, me).wait_send())

    def arrive(ref, sem):
        remote(ref, ref, sem, me).wait_recv()

    def send_shares(part, got, bits, w, sem):
        for n, mask in enumerate(masks_of(bits)):
            theirs = pl.ds(ordinal(bits, mask) * w, w)
            remote(part.at[theirs], got.at[n], sem, device(mask)).start()
        finish(got, sem)

    def send_all(ref, seen, bits, sem):
        for n, mask in enumerate(masks_of(bits)):
            remote(ref, seen.at[n], sem, device(mask)).start()
        finish(seen, sem)

    def send_mine(full, bits, w, sem):
        at = pl.ds(ordinal(bits) * w, w)
        for mask in masks_of(bits):
            remote(full.at[at], full.at[at], sem, device(mask)).start()
        finish(full.at[pl.ds(0, full.shape[0] - w)], sem)

    def combine(k, slot, beside=None, spare=None):
        level = LEVELS[k]
        w = level.share
        part, got, mine, seen = bufs[2 * k + slot][:4]
        s = 3 * (2 * k + slot)
        if not slot:
            send_shares(part, got, level.scatter, w, s)
        if beside:
            beside()
        arrive(got, s)
        mine[...] = part[pl.ds(ordinal(level.scatter) * w, w)] + jnp.sum(got[...], axis=0)
        return swap(k, slot, spare)

    def swap(k, slot, spare=None):
        mine, seen = bufs[2 * k + slot][2:4]
        s = 3 * (2 * k + slot) + 1
        send_all(mine, seen, LEVELS[k].exchange, s)
        if spare:
            spare()
        arrive(seen, s)
        return mine[...] + jnp.sum(seen[...], axis=0)

    def spread_out(k, slot, value):
        level = LEVELS[k]
        w = level.share
        full = bufs[2 * k + slot][4]
        s = 3 * (2 * k + slot) + 2
        full[pl.ds(ordinal(level.scatter) * w, w)] = value
        send_mine(full, level.scatter, w, s)
        arrive(full.at[pl.ds(0, level.tiles - w)], s)

    top_bits = LEVELS[0].scatter
    n_top = 1 << len(top_bits)

    def columns(mask=0):
        return pl.ds(pl.multiple_of(ordinal(top_bits, mask) * TILE, TILE), TILE)

    def send_columns():
        mine = cols.at[ordinal(top_bits)]
        pltpu.make_async_copy(f1_h.at[:, columns()], mine, in_sem.at[13]).start()
        for mask in masks_of(top_bits):
            remote(f1_h.at[:, columns(mask)], mine, 24, device(mask)).start()
        finish(cols.at[pl.ds(0, n_top - 1)], 24)

    def columns_here():
        pltpu.make_async_copy(f1_h.at[:, columns()], cols.at[ordinal(top_bits)], in_sem.at[13]).wait()
        arrive(cols.at[pl.ds(0, n_top - 1)], 24)

    def middle(tile):
        rows = n_top * LEVELS[0].own
        part = dense(tile, cols[...].reshape(rows, TILE), NT)
        zbuf, zgot, zmine, zseen, znext, zlast, zfull = mids
        n = rows // TILE
        for j in range(n):
            zbuf[j] = part[:, j * TILE : (j + 1) * TILE]
        w = n >> len(MID_SCATTER)
        at = pl.ds(ordinal(MID_SCATTER) * w, w)
        send_shares(zbuf, zgot, MID_SCATTER, w, 25)
        arrive(zgot, 25)
        zmine[...] = zbuf[at] + jnp.sum(zgot[...], axis=0)
        send_all(zmine, zseen, MID_EXCHANGES[0], 26)
        arrive(zseen, 26)
        znext[...] = zmine[...] + jnp.sum(zseen[...], axis=0)
        send_all(znext, zlast, MID_EXCHANGES[1], 28)
        arrive(zlast, 28)
        zfull[at] = znext[...] + jnp.sum(zlast[...], axis=0)
        send_mine(zfull, MID_SCATTER, w, 27)
        arrive(zfull.at[pl.ds(0, n - w)], 27)
        whole = jnp.concatenate([zfull[j] for j in range(n)], axis=1)
        return dense(whole, cols[...].reshape(rows, TILE))

    crowd = masks_of(SPARSE)
    n_crowd = len(crowd)
    early, terms, hots, owns, half, other, top = bufs[6]

    def introduce():
        for n, mask in enumerate(crowd):
            remote(early.at[n_crowd], early.at[n], 18, device(mask)).start()
        finish(early.at[pl.ds(0, n_crowd)], 18)

    def send_terms():
        for n, mask in enumerate(crowd):
            remote(terms.at[n_crowd], terms.at[n], 19, device(mask)).start()
        finish(terms.at[pl.ds(0, n_crowd)], 19)

    def meet():
        arrive(early.at[pl.ds(0, n_crowd)], 18)
        owns[...] = jnp.zeros_like(owns)
        for n, mask in enumerate(crowd + [0]):
            at = pl.ds(ordinal((2, 4, 5, 6), mask), 1)
            owns[at] = owns[at] + early[n, 0:8, :][None]
        lanes = lax.broadcasted_iota(jnp.int32, (TILE, TILE), 0).astype(F32)

        def body(n, _):
            row = early[n, 8:9, :]
            lane = row - TILE * jnp.floor(row * (1.0 / TILE))
            hots[n] = jnp.where(jnp.broadcast_to(lane, (TILE, TILE)) == lanes, 1.0, 0.0).astype(BF16)
            return 0

        lax.fori_loop(0, n_crowd + 1, body, 0, unroll=4)

    def add_terms():
        arrive(terms.at[pl.ds(0, n_crowd)], 19)
        tiles = LEVELS[3].tiles
        counts = lax.broadcasted_iota(jnp.int32, (tiles, 8, TILE), 0).astype(F32)

        def one(n):
            tile = jnp.floor(early[n, 8:9, :] * (1.0 / TILE))
            hit = jnp.broadcast_to(tile[None], (tiles, 8, TILE)) == counts
            return jnp.concatenate(
                [
                    jnp.where(hit, jnp.broadcast_to(v[None], (tiles, 8, TILE)), 0.0).reshape(tiles * 8, TILE)
                    for v in halves(terms[n])
                ],
                axis=0,
            ).astype(BF16)

        def body(g, total):
            left = jnp.concatenate([one(2 * g), one(2 * g + 1)], axis=1)
            right = jnp.concatenate([hots[2 * g], hots[2 * g + 1]], axis=1)
            return total + fast(left, right, NT)

        both = lax.fori_loop(0, (n_crowd + 1) // 2, body, jnp.zeros((tiles * 16, TILE), F32), unroll=8)
        half[...] = owns[...] + (both[: tiles * 8] + both[tiles * 8 :]).reshape(tiles, 8, TILE)
        remote(half, other, 20, device(1 << 4)).start()
        finish(half, 20)
        arrive(other, 20)
        top[...] = half[...] + other[...]

    def times_rows(k, full):
        factor = factors[k]
        m = LEVELS[k].own

        def body(j, sums):
            tile = full[j]
            rows = factor[:, pl.ds(pl.multiple_of(j * TILE, TILE), TILE)]
            return tuple(sums[q] + tile * rows[q : q + 1, :] for q in range(m))

        sums = lax.fori_loop(0, LEVELS[k].tiles, body, tuple(jnp.zeros((8, TILE), F32) for _ in range(m)), unroll=16)
        return [jnp.sum(v, axis=1, keepdims=True) for v in sums]

    def spread_share(k, wide, out, place):
        factor = factors[k]
        w = LEVELS[k].share
        for j in range(w):
            tile = place * w + j
            rows = factor[:, pl.ds(pl.multiple_of(tile * TILE, TILE), TILE)]
            acc = wide[0] * rows[0:1, :]
            for q in range(1, LEVELS[k].own):
                acc = acc + wide[q] * rows[q : q + 1, :]
            out[tile] = acc

    def spread_send(k, values):
        part, got = bufs[2 * k + 1][:2]
        bits = LEVELS[k].scatter
        w = LEVELS[k].share
        s = 3 * (2 * k + 1)
        wide = [jnp.broadcast_to(v, (8, TILE)) for v in values]
        for n, mask in enumerate(masks_of(bits)):
            place = ordinal(bits, mask)
            spread_share(k, wide, part, place)
            remote(part.at[pl.ds(place * w, w)], got.at[n], s, device(mask)).start()
        spread_share(k, wide, part, ordinal(bits))
        finish(got, s)

    def spread(k, values, out):
        factor = factors[k]
        m = LEVELS[k].own
        wide = [jnp.broadcast_to(v, (8, TILE)) for v in values]

        def body(j, _):
            rows = factor[:, pl.ds(pl.multiple_of(j * TILE, TILE), TILE)]
            acc = wide[0] * rows[0:1, :]
            for q in range(1, m):
                acc = acc + wide[q] * rows[q : q + 1, :]
            out[j] = acc
            return 0

        lax.fori_loop(0, LEVELS[k].tiles, body, 0, unroll=4)

    def inverse_blocks():
        vmat[...] = jnp.zeros_like(vmat)
        for j in range(4):
            vmat[j * TILE : (j + 1) * TILE, j * TILE : (j + 1) * TILE] = inv[j]
        for j in (2, 1, 0):
            step = -dense(inv[j], sub[j])
            vmat[j * TILE : (j + 1) * TILE, (j + 1) * TILE :] = dense(
                step, vmat[(j + 1) * TILE : (j + 2) * TILE, (j + 1) * TILE :]
            )

    def coupled():
        cv[...] = dense(cpl[3], vmat[...], NT)

    for n in range(6):
        copies[n].wait()
    early[n_crowd, 0:8, :] = dense(sep[...], select(3))
    early[n_crowd, 8:9, :] = pos[3:4, :].astype(F32)
    earlier = None
    for j in range(4):
        current = rhs[:, j * TILE : (j + 1) * TILE]
        if j:
            current = current - dense(earlier, sub[j - 1])
        earlier = dense(current, inv[j])
        fwd[:, j * TILE : (j + 1) * TILE] = earlier
    terms[n_crowd] = -dense(fwd[...], cpl[3], NT)
    pl.semaphore_wait(barrier, len(greet))
    introduce()
    send_terms()
    meet()
    copies[6].wait()
    prepare(2)
    copies[7].wait()
    copies[8].wait()
    add_terms()

    def beside_three():
        prepare(1)
        prepare(0)
        prepare(3)
        inverse_blocks()

    values = None
    for k in (3, 2, 1, 0):
        m = LEVELS[k].own
        full = top
        if k == 2:
            value = combine(2, 0, beside_three, send_columns)
        elif k == 1:
            value = combine(1, 0)
        elif k == 0:
            bufs[1][2][...] = middle(combine(0, 0, coupled, columns_here)[0])[None]
            break
        if k < 3:
            spread_out(k, 0, value)
            full = bufs[2 * k][4]
            copies[{2: 9, 1: 11}[k]].wait()
            copies[{2: 10, 1: 12}[k]].wait()
        values = times_rows(k, full)
        term = base[k - 1]
        for q in range(m):
            term = term + values[q] * links[k - 1][q : q + 1, :]
        scatter(k - 1, term, bufs[2 * (k - 1)][0])
        for q in range(m):
            zval[LEVELS[k].off + q] = jnp.broadcast_to(values[q], (8, TILE))

    picked = None
    for k in range(4):
        m = LEVELS[k].own
        if k:
            values = [
                zval[LEVELS[k].off + q]
                - jnp.sum(picked * links[k - 1][q : q + 1, :], axis=1, keepdims=True)
                for q in range(m)
            ]
            spread_send(k, values)

        def after(k=k, picked=picked):
            if k == 0:
                work[...] = fwd[...]
                sep_out[...] = jnp.zeros_like(sep_out)
                return
            work[...] = work[...] - dense(picked, cpl[k - 1])
            sep_out[...] = sep_out[...] + dense(bufs[2 * k - 1][4][pl.ds(own_tile(k - 1), 1)][0], select(k - 1), NT)
            if k == 3:
                work[...] = dense(work[...], vmat[...], NT)

        value = combine(k, 1, after) if k else swap(0, 1, after)
        spread_out(k, 1, value)
        picked = gather(k, bufs[2 * k + 1][4])
    leaf_out[...] = work[...] - dense(picked, cv[...])
    sep_out[...] = sep_out[...] + dense(bufs[7][4][pl.ds(own_tile(3), 1)][0], select(3), NT)
    for sent in leftover:
        sent()


def local(*args):
    ins = [x[0, 0] for x in args]
    vmem = [pltpu.VMEM(x.shape, x.dtype) for n, x in enumerate(ins) if n != 6]
    bufs = []
    for k, level in enumerate(LEVELS):
        w = level.share
        n_crowd = 1 << len(SPARSE)
        shapes = (
            (level.tiles, 8, TILE),
            ((1 << len(level.scatter)) - 1, w, 8, TILE),
            (w, 8, TILE),
            ((1 << len(level.exchange)) - 1, w, 8, TILE),
            (level.tiles, 8, TILE),
        )
        usual = tuple(pltpu.VMEM(s, F32) for s in shapes)
        whole = pltpu.VMEM((level.tiles, 8, TILE), F32)
        if k == 3:
            bufs.append(
                (
                    pltpu.VMEM((n_crowd, 9, TILE), F32),
                    pltpu.VMEM((n_crowd, 8, TILE), F32),
                    pltpu.VMEM((n_crowd, TILE, TILE), BF16),
                    whole,
                    whole,
                    whole,
                    whole,
                )
            )
        else:
            bufs.append(usual)
        bufs.append(usual)
    scratch = vmem + [
        pltpu.VMEM((8, 512), F32),
        pltpu.VMEM((4, 8, TILE), F32),
        pltpu.VMEM((4, 2 * TILE, TILE), BF16),
        pltpu.VMEM((4, 2 * TILE, TILE), BF16),
        pltpu.VMEM((4, 8, TILE), F32),
        pltpu.VMEM((96, 8, TILE), F32),
        pltpu.VMEM((512, 512), F32),
        pltpu.VMEM((TILE, 512), F32),
        pltpu.VMEM((8, 512), F32),
        pltpu.VMEM((1 << len(LEVELS[0].scatter), LEVELS[0].own, TILE), F32),
    ]
    n = (LEVELS[0].own << len(LEVELS[0].scatter)) // TILE
    w = n >> len(MID_SCATTER)
    mids = tuple(
        pltpu.VMEM(s + (8, TILE), F32)
        for s in (
            (n,),
            ((1 << len(MID_SCATTER)) - 1, w),
            (w,),
            ((1 << len(MID_EXCHANGES[0])) - 1, w),
            (w,),
            ((1 << len(MID_EXCHANGES[1])) - 1, w),
            (n,),
        )
    )
    sems = (
        pltpu.SemaphoreType.DMA((14,)),
        pltpu.SemaphoreType.DMA((32,)),
        pltpu.SemaphoreType.DMA((32,)),
    )
    leaf, sep = pl.pallas_call(
        kernel,
        out_shape=(jax.ShapeDtypeStruct((8, 512), F32), jax.ShapeDtypeStruct((8, 96), F32)),
        in_specs=[pl.BlockSpec(memory_space=pltpu.HBM)] * len(ins),
        out_specs=(pl.BlockSpec(memory_space=pltpu.VMEM),) * 2,
        scratch_shapes=scratch + bufs + [mids, sems],
        compiler_params=pltpu.CompilerParams(
            collective_id=0, has_side_effects=True, vmem_limit_bytes=60 * 1024 * 1024
        ),
        name="nested_solve",
    )(*ins)
    return leaf[None, None], sep[None, None]


def solution(mesh):
    four = P("gx", "gy", None, None)
    five = P("gx", "gy", None, None, None)
    in_specs = (four, five, five, four, four, five) + (four,) * 7
    return jax.shard_map(local, mesh=mesh, in_specs=in_specs, out_specs=(four, four), check_vma=False)
```
